32 devices in a mesh: dp: 16 (over z, y, x), cores: 2 (over core).
Axes of the slice: x: 2, y: 2, z: 4, core: 2. Of those that a mesh axis runs over, the one named last changes fastest.
Arguments:
- queries: bfloat16 [16384, 1024], P(('dp', 'cores')), may hold values from -4 to 4
- passages: bfloat16 [16384, 1024], P(('dp', 'cores')), may hold values from -4 to 4
- positives: int32 [32, 512], P(('dp', 'cores')), may hold values from 0 to 511, each once within a row
- pair_blocks: int32 [32, 8], P(('dp', 'cores')), may hold values from 0 to 31, as said below
- negative_pair_count: int32 [32], P(('dp', 'cores')), may hold values from 1 to 8, as said below
Outputs:
- query_loss: float32 [32, 512], P(('dp', 'cores'))
- passage_loss: float32 [32, 512], P(('dp', 'cores'))
- query_grad: float32 [16384, 1024], P(('dp', 'cores'))
- passage_grad: float32 [16384, 1024], P(('dp', 'cores'))
The draws below stay inside these ranges and needn't reach their ends.
Inputs may be any that keep to these rules, and one draw needn't show every extreme that they name: `pair_blocks`: row b lists 8 different blocks, each (b + o) mod 32 with 1 <= |o| <= 4, so every block within 4 of b in cyclic order appears once. `negative_pair_count`: some block has 8 hard negatives and some block has 1 in every draw.
All inputs are finite; a program needn't handle non-finite values.
Results may differ from the reference program's by a relative error of at most 0.0022.
Values may be sent and summed in bfloat16 or wider, within the bound.
A program may use at most 128 MiB of HBM per device.

```python
import math
import jax
import jax.numpy as jnp
from jax import lax

D = 1024
BLK = 512
RANGE = 4
NEG = 8
NB = 32
ROWS = 16384


def newly_arrived_entries(key, low, high):
    scale = jnp.exp(jax.random.uniform(jax.random.fold_in(key, 2), (ROWS, 1), jnp.float32, math.log(low), math.log(high)))
    values = jax.random.truncated_normal(key, -5.0, 5.0, (ROWS, D), jnp.float32)
    return scale * values / math.sqrt(D)


def embeddings(key, constant):
    key = jax.random.fold_in(key, constant)
    values = newly_arrived_entries(key, 0.5, 2.5)
    return values.astype(jnp.bfloat16)


def draw_queries(key, part):
    return embeddings(key, 11)


def draw_passages(key, part):
    return embeddings(key, 17)


def draw_pair_blocks(key, part):
    key = jax.random.fold_in(key, 31)
    keys = jax.random.split(key, NB)
    offsets = jnp.concatenate([jnp.arange(-RANGE, 0), jnp.arange(1, RANGE + 1)]).astype(jnp.int32)
    order = jax.vmap(lambda lone_example: jax.random.permutation(lone_example, offsets))(keys)
    return ((jnp.arange(NB, dtype=jnp.int32)[:, None] + order) % NB).astype(jnp.int32)


def draw_negative_pair_count(key, part):
    key = jax.random.fold_in(key, 41)
    count = jax.random.randint(key, (NB,), 1, NEG + 1).astype(jnp.int32)
    chosen_passage = jax.random.randint(jax.random.fold_in(key, 1), (), 0, NB)
    count = count.at[chosen_passage].set(NEG)
    count = count.at[(chosen_passage + 1) % NB].set(1)
    return count.astype(jnp.int32)


def setup_inputs(seed: int = 0) -> dict:
    seeds = jax.random.split(jax.random.key(seed), 6)
    queries = draw_queries(jax.random.fold_in(seeds[5], 71), 0)
    passages = draw_passages(jax.random.fold_in(seeds[5], 71), 0)
    positives = jax.vmap(lambda own: jax.random.permutation(own, BLK))(jax.random.split(seeds[2], NB)).reshape((NB, BLK)).astype(jnp.int32)
    pair_blocks = draw_pair_blocks(jax.random.fold_in(seeds[5], 71), 0)
    negative_pair_count = draw_negative_pair_count(jax.random.fold_in(seeds[5], 71), 0)
    return dict(queries=queries, passages=passages, positives=positives, pair_blocks=pair_blocks, negative_pair_count=negative_pair_count)


logit_multiplier = 20.0
far_negative = -1.0e30


def slot_offsets(reach):
    return [0] + [offset for offset in range(-reach, reach + 1) if offset != 0]


def slot_mask(pair_blocks, negative_pair_count, block_ids, blocks, reach):
    listed = pair_blocks.shape[1]
    used = jnp.arange(listed, dtype=jnp.int32)[None, :] < negative_pair_count[:, None]
    columns = []
    for offset in slot_offsets(reach):
        if offset == 0:
            columns.append(jnp.ones(block_ids.shape, dtype=bool))
        else:
            target = (block_ids + offset) % blocks
            columns.append(jnp.any((pair_blocks == target[:, None]) & used, axis=1))
    return jnp.stack(columns, axis=1)


def scores_of(query_rows, passage_rows):
    plain_similarities = lax.dot_general(query_rows, passage_rows, (((1,), (1,)), ((), ())), preferred_element_type=jnp.float32)
    return logit_multiplier * plain_similarities


def partial_stats(scores):
    row_top = jnp.max(scores, axis=1)
    line_exponential_sum = jnp.sum(jnp.exp(scores - row_top[:, None]), axis=1)
    col_top = jnp.max(scores, axis=0)
    col_total = jnp.sum(jnp.exp(scores - col_top[None, :]), axis=0)
    return row_top, line_exponential_sum, col_top, col_total


def merge_lse(tops, totals):
    top = jnp.max(tops, axis=0)
    return top + jnp.log(jnp.sum(totals * jnp.exp(tops - top), axis=0))


def weight_of(scores, row_lse, col_lse, present_markers, diagonal):
    similarity_gap = jnp.exp(scores - row_lse[:, None]) + jnp.exp(scores - col_lse[None, :])
    if diagonal is not None:
        similarity_gap = similarity_gap - 2.0 * diagonal
    return jnp.where(present_markers, logit_multiplier * similarity_gap, 0.0).astype(jnp.bfloat16)


def reference(queries, passages, positives, pair_blocks, negative_pair_count):
    query_blocks = queries.reshape(NB, BLK, D)
    passage_blocks = passages.reshape(NB, BLK, D)
    block_ids = jnp.arange(NB, dtype=jnp.int32)
    mask = slot_mask(pair_blocks, negative_pair_count, block_ids, NB, RANGE)
    offsets = slot_offsets(RANGE)
    columns = jnp.arange(BLK, dtype=jnp.int32)

    def first(block):
        query_rows = query_blocks[block]
        diagonal = (positives[block][:, None] == columns[None, :]).astype(jnp.float32)
        tops, totals, col_tops, col_totals = [], [], [], []
        row_pos = None
        col_pos = None
        for slot, offset in enumerate(offsets):
            target = (block + offset) % NB
            scores = scores_of(query_rows, passage_blocks[target])
            row_top, line_exponential_sum, col_top, col_total = partial_stats(scores)
            present_markers = mask[block, slot]
            tops.append(jnp.where(present_markers, row_top, far_negative))
            totals.append(jnp.where(present_markers, line_exponential_sum, 0.0))
            col_tops.append(jnp.where(present_markers, col_top, far_negative))
            col_totals.append(jnp.where(present_markers, col_total, 0.0))
            if offset == 0:
                row_pos = jnp.sum(scores * diagonal, axis=1)
                col_pos = jnp.sum(scores * diagonal, axis=0)
        row_lse = merge_lse(jnp.stack(tops), jnp.stack(totals))
        return row_lse, row_pos, col_pos, jnp.stack(col_tops), jnp.stack(col_totals)

    row_lse, row_pos, col_pos, col_tops, col_totals = lax.map(first, block_ids)
    shifted_tops = jnp.stack([jnp.roll(col_tops[:, slot], offset, axis=0) for slot, offset in enumerate(offsets)])
    shifted_totals = jnp.stack([jnp.roll(col_totals[:, slot], offset, axis=0) for slot, offset in enumerate(offsets)])
    col_lse = merge_lse(shifted_tops, shifted_totals)
    query_loss = row_lse - row_pos
    passage_loss = col_lse - col_pos

    def latter_operand(passage_grad, block):
        query_rows = query_blocks[block]
        diagonal = (positives[block][:, None] == columns[None, :]).astype(jnp.float32)
        query_grad = jnp.zeros((BLK, D), jnp.float32)
        for slot, offset in enumerate(offsets):
            target = (block + offset) % NB
            passage_rows = passage_blocks[target]
            scores = scores_of(query_rows, passage_rows)
            weight = weight_of(scores, row_lse[block], col_lse[target], mask[block, slot], diagonal if offset == 0 else None)
            query_grad = query_grad + jnp.dot(weight, passage_rows, preferred_element_type=jnp.float32)
            term = lax.dot_general(weight, query_rows, (((0,), (0,)), ((), ())), preferred_element_type=jnp.float32)
            passage_grad = passage_grad.at[target].add(term)
        return passage_grad, query_grad

    passage_grad, query_grad = lax.scan(latter_operand, jnp.zeros((NB, BLK, D), jnp.float32), block_ids)
    return query_loss, passage_loss, query_grad.reshape(ROWS, D), passage_grad.reshape(ROWS, D)
```

```python
import functools

import jax
import jax.numpy as jnp
from jax import lax
from jax.experimental import pallas as pl
from jax.experimental.pallas import tpu as pltpu
from jax.sharding import PartitionSpec as P

RANGE = 4
OWN = RANGE
SLOTS = 2 * RANGE + 1
MESH = pl.DeviceIdType.MESH
SCALE = 20.0
FAR = -1.0e30

NT = (((1,), (1,)), ((), ()))


def kernel(chips, q_hbm, p_hbm, bias_ref, pos_col, pos_row, gq_ref, gp_ref, loss_ref,
           buf, relay, sc, tops, totals, bbuf, lbuf,
           load_sem, send_sem, recv_sem, relay_sem, bsend, brecv, lsend, lrecv):
    chip = lax.axis_index("dp")
    core = lax.axis_index("cores")
    me = 2 * chip + core
    blocks = 2 * chips
    j = chip % 4
    sigma = 1 - 2 * (j // 2)
    is_a = 1 - ((j + 1) // 2) % 2
    tau = sigma * (2 * is_a - 1)
    which = j // 2

    def device(block):
        block = (block + blocks) % blocks
        return (block // 2, block % 2)

    sibling = (chip, 1 - core)
    x_dev = ((chip + tau + chips) % chips, core)
    y_dev = ((chip + 2 * sigma + chips) % chips, core)
    z_dev = ((chip + 4 * sigma + chips) % chips, core)

    def at(k):
        return OWN + 2 * k

    xs, ys, zs, fs = at(tau), at(2 * sigma), at(-2 * sigma), at(-tau)
    turn = 1 - 2 * core

    loads = [
        pltpu.make_async_copy(q_hbm, buf.at[OWN, 0], load_sem.at[0]),
        pltpu.make_async_copy(p_hbm, buf.at[OWN, 1], load_sem.at[1]),
    ]
    for load in loads:
        load.start()

    barrier = pltpu.get_barrier_semaphore()
    others = [o for o in range(-RANGE, RANGE + 1) if o != 0]
    greeted = others + [-8, 8]
    for o in greeted:
        pl.semaphore_signal(barrier, inc=1, device_id=device(me + o), device_id_type=MESH)
    bbuf[OWN] = bias_ref[...]
    for load in loads:
        load.wait()
    pl.semaphore_wait(barrier, len(greeted))

    def put(src, dst, to, sent, got):
        return pltpu.make_async_remote_copy(
            src_ref=src, dst_ref=dst, send_sem=sent, recv_sem=got, device_id=to, device_id_type=MESH
        )

    def block(slot, m, to, to_slot, n):
        return put(buf.at[slot, m], buf.at[to_slot, m], to, send_sem.at[n], recv_sem.at[to_slot, m])

    def bias_copy(o):
        slot = OWN - o
        return put(bbuf.at[OWN], bbuf.at[slot], device(me + o), bsend.at[OWN + o], brecv.at[slot])

    def lse_copy(o):
        slot = OWN - o
        return put(lbuf.at[OWN], lbuf.at[slot], device(me + o), lsend.at[OWN + o], lrecv.at[slot])

    own_x = [block(OWN, m, x_dev, at(-tau), m) for m in range(2)]
    own_y = [block(OWN, m, y_dev, at(-2 * sigma), 2 + m) for m in range(2)]
    own_s = [block(OWN, m, sibling, OWN - turn, 4 + m) for m in range(2)]
    for m in range(2):
        own_x[m].start()
        own_y[m].start()
        if m == 0:
            for o in others:
                bias_copy(o).start()
    for m in range(2):
        own_s[m].start()

    def forward(slot, m, n):
        return block(slot, m, sibling, slot - turn, n)

    def forwarded(slot):
        return jnp.logical_and(slot - turn >= 0, slot - turn < SLOTS)

    diag_y = [block(xs, m, y_dev, at(-sigma), 6) for m in range(2)]
    diag_x = [block(ys, m, x_dev, at(sigma), 7) for m in range(2)]
    to_z = [block(ys, m, z_dev, at(-2 * sigma), 8 + m) for m in range(2)]
    to_relay = put(buf.at[xs, 1], relay, y_dev, send_sem.at[10], relay_sem.at[0])
    from_relay = put(relay, buf.at[at(-sigma), 1], z_dev, send_sem.at[10], recv_sem.at[at(-sigma), 1])
    last_x = block(zs, 0, x_dev, at(-sigma), 11)

    tops[...] = jnp.full(tops.shape, FAR, jnp.float32)
    totals[...] = jnp.zeros(totals.shape, jnp.float32)

    sib = [s + turn for s in (OWN, xs, ys, zs, fs)]
    plan = [
        (OWN, 0), (OWN, 1), (sib[0], 0), (sib[0], 1),
        (xs, 0), (ys, 0), (xs, 1), (ys, 1),
        (sib[1], 0), (sib[2], 0), (sib[1], 1), (sib[2], 1),
        (zs, 0), (zs, 1), (fs, 0), (fs, 1),
        (sib[3], 0), (sib[3], 1), (sib[4], 0), (sib[4], 1),
    ]

    def event(e, carry):
        slot = jnp.int32(OWN)
        m = jnp.int32(0)
        for i, (s, which_m) in enumerate(plan):
            slot = jnp.where(e == i, s, slot)
            m = jnp.where(e == i, which_m, m)
        present = jnp.logical_and(slot >= 0, slot < SLOTS)
        slot = jnp.where(present, slot, 0)
        side = 1 - m

        @pl.when(jnp.logical_and(e == 8, is_a == 1))
        def _():
            put(relay, relay, sibling, send_sem.at[10], relay_sem.at[0]).wait_recv()
            from_relay.start()

        @pl.when(jnp.logical_and(e > 1, present))
        def _():
            block(slot, m, sibling, slot, 0).wait_recv()

            @pl.when(m == 0)
            def _():
                put(bbuf.at[slot], bbuf.at[slot], sibling, bsend.at[0], brecv.at[slot]).wait_recv()

        for i in (5, 7):
            @pl.when(e == i)
            def _():
                to_z[i // 6].start()

                @pl.when(jnp.logical_and(is_a == 1, which == i // 6))
                def _():
                    diag_x[i // 6].start()

        for i in (4, 6):
            @pl.when(jnp.logical_and(jnp.logical_and(e == i, is_a == 1), which == i // 6))
            def _():
                diag_y[i // 6].start()

        @pl.when(jnp.logical_and(e == 6, is_a == 0))
        def _():
            to_relay.start()

        @pl.when(jnp.logical_and(e == 12, is_a == 0))
        def _():
            last_x.start()

        for i in (4, 5, 6, 7, 12, 13, 14, 15):
            s, which_m = plan[i]

            @pl.when(jnp.logical_and(e == i, forwarded(s)))
            def _():
                forward(s, which_m, 8 + i if i >= 12 else 12 + i - 4).start()

        @pl.when(present)
        def _():
            bias = bbuf[jnp.where(side == 0, OWN, slot), pl.ds(jnp.where(side == 0, slot, SLOTS - 1 - slot), 1), :]
            rows = buf.shape[2]
            for r in range(0, rows, rows // 2):
                part = pl.ds(r, rows // 2)
                s = SCALE * lax.dot_general(
                    buf[OWN, side, part, :], buf[slot, m], NT, preferred_element_type=jnp.float32
                ) + bias
                sc[slot, side, part, :] = s
                old = tops[side, part, :]
                top = jnp.maximum(old, jnp.max(s, axis=1, keepdims=True))
                total = totals[side, part, :] * jnp.exp(old - top)
                totals[side, part, :] = total + jnp.sum(jnp.exp(s - top), axis=1, keepdims=True)
                tops[side, part, :] = top

        return carry

    lax.fori_loop(0, len(plan), event, 0)

    rows = buf.shape[2]
    for side in range(2):
        lse = tops[side] + jnp.log(totals[side])
        tops[side] = lse
        lbuf[OWN, side] = jnp.transpose(jnp.broadcast_to(lse, (rows, 128)))[0:8]
    for o in others:
        lse_copy(o).start()

    grads = (gq_ref, gp_ref)

    def gradient(slot, side, own):
        other = lbuf[slot, 1 - side, 0:1, :]
        for r in range(0, rows, rows // 2):
            part = pl.ds(r, rows // 2)
            s = sc[slot, side, part, :]
            w = jnp.exp(s - tops[side, part, :]) + jnp.exp(s - other)
            if own:
                if side == 0:
                    hit = pos_col[part, :] == lax.broadcasted_iota(jnp.int32, s.shape, 1)
                else:
                    hit = pos_row[...] == lax.broadcasted_iota(jnp.int32, s.shape, 0) + r
                e = hit.astype(jnp.float32)
                w = w - 2.0 * e
                totals[side, part, :] = tops[side, part, :] - jnp.sum(s * e, axis=1, keepdims=True)
            w = (SCALE * w).astype(jnp.bfloat16)
            term = jnp.dot(w, buf[slot, 1 - side], preferred_element_type=jnp.float32)
            if own:
                grads[side][part, :] = term
            else:
                grads[side][part, :] += term

    for side in range(2):
        gradient(OWN, side, True)
        loss_ref[side] = jnp.transpose(jnp.broadcast_to(totals[side], (rows, 128)))[0:8]

    def later(t, carry):
        slot = t + t // RANGE
        put(lbuf.at[slot], lbuf.at[slot], sibling, lsend.at[0], lrecv.at[slot]).wait_recv()
        for side in range(2):
            gradient(slot, side, False)
        return carry

    lax.fori_loop(0, SLOTS - 1, later, 0)

    for copy in own_x + own_y + own_s + to_z:
        copy.wait_send()
    for i in (4, 5, 6, 7, 12, 13, 14, 15):
        s, which_m = plan[i]

        @pl.when(forwarded(s))
        def _():
            forward(s, which_m, 8 + i if i >= 12 else 12 + i - 4).wait_send()

    @pl.when(is_a == 1)
    def _():
        diag_y[0].wait_send()
        diag_x[0].wait_send()
        from_relay.wait_send()

    @pl.when(is_a == 0)
    def _():
        to_relay.wait_send()
        last_x.wait_send()

    for o in others:
        bias_copy(o).wait_send()
        lse_copy(o).wait_send()


def present_pairs(pair_blocks, negative_pair_count, block, blocks):
    listed = pair_blocks.shape[1]
    used = jnp.arange(listed, dtype=jnp.int32) < negative_pair_count[0]
    offsets = jnp.arange(-RANGE, RANGE + 1, dtype=jnp.int32)
    target = (block + offsets) % blocks
    found = jnp.any((pair_blocks[0][None, :] == target[:, None]) & used[None, :], axis=1)
    return found | (offsets == 0)


def solution(mesh):
    chips = mesh.shape["dp"]
    blocks = chips * mesh.shape["cores"]

    def body(queries, passages, positives, pair_blocks, negative_pair_count):
        rows, width = queries.shape
        block = lax.axis_index(("dp", "cores"))
        present = present_pairs(pair_blocks, negative_pair_count, block, blocks)
        bias = jnp.where(present, 0.0, FAR).astype(jnp.float32)
        bias = jnp.broadcast_to(jnp.pad(bias, (0, 16 - SLOTS))[:, None], (16, rows))
        vmem = pl.BlockSpec(memory_space=pltpu.VMEM)
        anywhere = pl.BlockSpec(memory_space=pl.ANY)
        gq, gp, loss = pl.pallas_call(
            functools.partial(kernel, chips),
            out_shape=(
                jax.ShapeDtypeStruct((rows, width), jnp.float32),
                jax.ShapeDtypeStruct((rows, width), jnp.float32),
                jax.ShapeDtypeStruct((2, 8, rows), jnp.float32),
            ),
            in_specs=[anywhere, anywhere, vmem, vmem, vmem],
            out_specs=(vmem, vmem, vmem),
            scratch_shapes=[
                pltpu.VMEM((SLOTS, 2, rows, width), jnp.bfloat16),
                pltpu.VMEM((rows, width), jnp.bfloat16),
                pltpu.VMEM((SLOTS, 2, rows, rows), jnp.float32),
                pltpu.VMEM((2, rows, 1), jnp.float32),
                pltpu.VMEM((2, rows, 1), jnp.float32),
                pltpu.VMEM((SLOTS, 16, rows), jnp.float32),
                pltpu.VMEM((SLOTS, 2, 8, rows), jnp.float32),
                pltpu.SemaphoreType.DMA((2,)),
                pltpu.SemaphoreType.DMA((24,)),
                pltpu.SemaphoreType.DMA((SLOTS, 2)),
                pltpu.SemaphoreType.DMA((1,)),
                pltpu.SemaphoreType.DMA((SLOTS,)),
                pltpu.SemaphoreType.DMA((SLOTS,)),
                pltpu.SemaphoreType.DMA((SLOTS,)),
                pltpu.SemaphoreType.DMA((SLOTS,)),
            ],
            compiler_params=pltpu.CompilerParams(
                collective_id=0, has_side_effects=True, vmem_limit_bytes=58 * 2**20
            ),
            cost_estimate=pl.CostEstimate(
                flops=36 * 2 * rows * rows * width,
                bytes_accessed=12 * rows * width,
                transcendentals=54 * rows * rows,
            ),
        )(queries, passages, bias, positives.reshape(rows, 1), positives)
        return loss[0, 0:1], loss[1, 0:1], gq, gp

    split = P(("dp", "cores"), None)
    return jax.shard_map(
        body,
        mesh=mesh,
        in_specs=(split, split, split, split, P(("dp", "cores"))),
        out_specs=(split, split, split, split),
        check_vma=False,
    )
```

```python
import functools

import jax
import jax.numpy as jnp
from jax import lax
from jax.experimental import pallas as pl
from jax.experimental.pallas import tpu as pltpu
from jax.sharding import PartitionSpec as P

RANGE = 4
OWN = RANGE
SLOTS = 2 * RANGE + 1
PASSING = SLOTS
MESH = pl.DeviceIdType.MESH
SCALE = 20.0
FAR = -1.0e30

NT = (((1,), (1,)), ((), ()))


def kernel(chips, q_hbm, p_hbm, bias_ref, pos_col, pos_row, gq_ref, gp_ref, loss_ref,
           buf, sc, tops, totals, bbuf, lbuf,
           load_sem, send_sem, recv_sem, bsend, brecv, lsend, lrecv):
    chip = lax.axis_index("dp")
    core = lax.axis_index("cores")
    me = 2 * chip + core
    blocks = 2 * chips
    j = chip % 4
    sigma = 1 - 2 * (j // 2)
    corner = ((j + 1) // 2) % 2 == 0
    tau = jnp.where(corner, sigma, -sigma)
    across = j // 2

    def device(block):
        block = (block + blocks) % blocks
        return (block // 2, block % 2)

    sibling = (chip, 1 - core)
    x_dev = ((chip + tau + chips) % chips, core)
    y_dev = ((chip + 2 * sigma + chips) % chips, core)
    z_dev = ((chip + 4 * sigma + chips) % chips, core)

    def at(k):
        return OWN + 2 * k

    xs, ys, zs, fs = at(tau), at(2 * sigma), at(-2 * sigma), at(-tau)
    turn = 1 - 2 * core
    half = buf.shape[3]
    rows = 2 * half

    loads = []
    for m, ref in enumerate((q_hbm, p_hbm)):
        for h in range(2):
            loads.append(pltpu.make_async_copy(
                ref.at[pl.ds(h * half, half)], buf.at[OWN, m, h], load_sem.at[2 * m + h]))
    for load in loads:
        load.start()

    barrier = pltpu.get_barrier_semaphore()
    others = [o for o in range(-RANGE, RANGE + 1) if o != 0]
    greeted = others + [-8, 8]
    for o in greeted:
        pl.semaphore_signal(barrier, inc=1, device_id=device(me + o), device_id_type=MESH)
    bbuf[OWN] = bias_ref[...]
    for load in loads:
        load.wait()
    pl.semaphore_wait(barrier, len(greeted))

    def put(src, dst, to, sent, got):
        return pltpu.make_async_remote_copy(
            src_ref=src, dst_ref=dst, send_sem=sent, recv_sem=got, device_id=to, device_id_type=MESH
        )

    def piece(slot, m, h, to, to_slot, n):
        return put(buf.at[slot, m, h], buf.at[to_slot, m, h], to, send_sem.at[n], recv_sem.at[to_slot, m, h])

    def arrival(slot, m, h):
        return piece(slot, m, h, sibling, slot, 0)

    def bias_copy(o):
        slot = OWN - o
        return put(bbuf.at[OWN], bbuf.at[slot], device(me + o), bsend.at[OWN + o], brecv.at[slot])

    def bias_arrival(slot):
        return put(bbuf.at[slot], bbuf.at[slot], sibling, bsend.at[0], brecv.at[slot])

    def lse_copy(o):
        slot = OWN - o
        return put(lbuf.at[OWN], lbuf.at[slot], device(me + o), lsend.at[OWN + o], lrecv.at[slot])

    def choose(a, b):
        return tuple(jnp.where(corner, u, v) for u, v in zip(a, b))

    x_out = [
        choose((OWN, 1, at(-tau)), (OWN, j - 1, at(-tau))),
        choose((OWN, 0, at(-tau)), (OWN, 2 - j, at(-tau))),
        choose((ys, across, at(sigma)), (zs, 0, at(-sigma))),
    ]
    y_out = [
        choose((OWN, 0, at(-2 * sigma)), (OWN, 2 - j, at(-2 * sigma))),
        choose((OWN, 1, at(-2 * sigma)), (xs, 1, PASSING)),
        choose((xs, across, at(-sigma)), (OWN, j - 1, at(-2 * sigma))),
    ]
    x_in = [
        choose((xs, across), (xs, 1)),
        choose((xs, 1 - across), (xs, 0)),
        choose((fs, 0), (fs, j - 1)),
    ]
    y_in = [
        choose((ys, across), (ys, 0)),
        choose((PASSING, 1), (ys, 1)),
        choose((ys, 1 - across), (fs, 2 - j)),
    ]
    z_in = [
        choose((zs, across), (zs, 0)),
        choose((fs, 1), (zs, 1)),
        choose((zs, 1 - across), (zs, 1)),
    ]

    def pick(groups, i):
        g = i // 2
        return tuple(jnp.where(g == 0, a, jnp.where(g == 1, b, c)) for a, b, c in zip(*groups))

    def x_send(i):
        slot, m, there = pick(x_out, i)
        return piece(slot, m, i % 2, x_dev, there, i)

    def y_send(i):
        slot, m, there = pick(y_out, i)
        return piece(slot, m, i % 2, y_dev, there, 6 + i)

    def z_send(i):
        slot, m = pick(y_in, i)
        there = jnp.where(slot == PASSING, at(-sigma), at(-2 * sigma))
        return piece(slot, m, i % 2, z_dev, there, 12 + i)

    def z_count():
        return jnp.where(corner, 6, 4)

    def shared(slot, step):
        there = slot + step
        return jnp.logical_and(jnp.logical_and(there >= 0, there < SLOTS), slot != PASSING)

    def forward(groups, i, n):
        slot, m = pick(groups, i)
        return shared(slot, -turn), piece(slot, m, i % 2, sibling, jnp.where(shared(slot, -turn), slot - turn, 0), n + i)

    for i in range(2):
        x_send(i).start()
        y_send(i).start()
    for o in others:
        bias_copy(o).start()
    own_s = [piece(OWN, m, h, sibling, OWN - turn, 36 + 2 * m + h) for m in range(2) for h in range(2)]
    for copy in own_s:
        copy.start()

    tops[...] = jnp.full(tops.shape, FAR, jnp.float32)
    totals[...] = jnp.zeros(totals.shape, jnp.float32)

    def score(slot, m, h):
        side = 1 - m
        bias = bbuf[jnp.where(side == 0, OWN, slot), pl.ds(jnp.where(side == 0, slot, SLOTS - 1 - slot), 1), :]
        bias = bias[:, :half]
        right = buf[slot, m, h]
        for r in range(2):
            part = pl.ds(r * half, half)
            s = SCALE * lax.dot_general(
                buf[OWN, side, r], right, NT, preferred_element_type=jnp.float32
            ) + bias
            sc[slot, side, h, part, :] = s
            old = tops[side, part, :]
            top = jnp.maximum(old, jnp.max(s, axis=1, keepdims=True))
            total = totals[side, part, :] * jnp.exp(old - top)
            totals[side, part, :] = total + jnp.sum(jnp.exp(s - top), axis=1, keepdims=True)
            tops[side, part, :] = top

    def own(e, carry):
        score(OWN, e // 2, e % 2)
        return carry

    def beside(e, carry):
        arrival(OWN + turn, e // 2, e % 2).wait_recv()
        score(OWN + turn, e // 2, e % 2)
        return carry

    lax.fori_loop(0, 4, own, 0)
    for o in others:
        bias_arrival(OWN - o).wait_recv()
    lax.fori_loop(0, 4, beside, 0)

    def step(t, carry):
        @pl.when(t < 6)
        def _():
            slot, m = pick(x_in, t)
            arrival(slot, m, t % 2).wait_recv()

            @pl.when(t < 4)
            def _():
                x_send(t + 2).start()

            slot, m = pick(y_in, t)
            arrival(slot, m, t % 2).wait_recv()

            @pl.when(t < z_count())
            def _():
                z_send(t).start()

            @pl.when(t < 4)
            def _():
                y_send(t + 2).start()

            for groups, n in ((x_in, 18), (y_in, 24)):
                used, copy = forward(groups, t, n)

                @pl.when(used)
                def _():
                    copy.start()

        @pl.when(jnp.logical_and(t >= 1, t - 1 < z_count()))
        def _():
            slot, m = pick(z_in, t - 1)
            arrival(slot, m, (t - 1) % 2).wait_recv()
            used, copy = forward(z_in, t - 1, 30)

            @pl.when(used)
            def _():
                copy.start()

        def sub(u, carry):
            link = u % 3
            beside = u // 3
            i = t - beside - jnp.where(link == 2, 1, 0)
            near = jnp.logical_and(i >= 0, i < jnp.where(link == 2, z_count(), 6))
            i = jnp.where(near, i, 0)
            slot, m = (
                jnp.where(link == 0, a, jnp.where(link == 1, b, c))
                for a, b, c in zip(pick(x_in, i), pick(y_in, i), pick(z_in, i))
            )
            moved = jnp.where(beside == 1, turn, 0)
            near = jnp.logical_and(near, shared(slot, moved))
            slot = jnp.where(near, slot + moved, 0)

            @pl.when(near)
            def _():
                @pl.when(beside == 1)
                def _():
                    arrival(slot, m, i % 2).wait_recv()

                score(slot, m, i % 2)

            return carry

        lax.fori_loop(0, 6, sub, 0)
        return carry

    lax.fori_loop(0, 8, step, 0)

    for side in range(2):
        lse = tops[side] + jnp.log(totals[side])
        tops[side] = lse
        lbuf[OWN, side] = jnp.transpose(jnp.broadcast_to(lse, (rows, 128)))[0:8]
    for o in others:
        lse_copy(o).start()

    grads = (gq_ref, gp_ref)

    def weight(slot, side, part):
        s = jnp.concatenate([sc[slot, side, h, part, :] for h in range(2)], axis=1)
        w = jnp.exp(s - tops[side, part, :]) + jnp.exp(s - lbuf[slot, 1 - side, 0:1, :])
        return s, w

    def product(w, slot, side):
        right = buf[slot, 1 - side].reshape(rows, buf.shape[4])
        return jnp.dot((SCALE * w).astype(jnp.bfloat16), right, preferred_element_type=jnp.float32)

    for side in range(2):
        for r in range(0, rows, half):
            part = pl.ds(r, half)
            s, w = weight(OWN, side, part)
            if side == 0:
                hit = pos_col[part, :] == lax.broadcasted_iota(jnp.int32, s.shape, 1)
            else:
                hit = pos_row[...] == lax.broadcasted_iota(jnp.int32, s.shape, 0) + r
            e = hit.astype(jnp.float32)
            totals[side, part, :] = tops[side, part, :] - jnp.sum(s * e, axis=1, keepdims=True)
            grads[side][part, :] = product(w - 2.0 * e, OWN, side)
        loss_ref[side] = jnp.transpose(jnp.broadcast_to(totals[side], (rows, 128)))[0:8]

    def later(t, carry):
        pair = (t, SLOTS - 1 - t)
        for slot in pair:
            put(lbuf.at[slot], lbuf.at[slot], sibling, lsend.at[0], lrecv.at[slot]).wait_recv()
        for side in range(2):
            for r in range(0, rows, half):
                part = pl.ds(r, half)
                terms = [product(weight(slot, side, part)[1], slot, side) for slot in pair]
                grads[side][part, :] += terms[0] + terms[1]
        return carry

    lax.fori_loop(0, RANGE, later, 0)

    for copy in own_s:
        copy.wait_send()

    def sent(i, carry):
        x_send(i).wait_send()
        y_send(i).wait_send()
        for groups, n, count in ((x_in, 18, 6), (y_in, 24, 6), (z_in, 30, z_count())):
            used, copy = forward(groups, i, n)

            @pl.when(jnp.logical_and(used, i < count))
            def _():
                copy.wait_send()

        @pl.when(i < z_count())
        def _():
            z_send(i).wait_send()

        return carry

    lax.fori_loop(0, 6, sent, 0)
    for o in others:
        bias_copy(o).wait_send()
        lse_copy(o).wait_send()


def present_pairs(pair_blocks, negative_pair_count, block, blocks):
    listed = pair_blocks.shape[1]
    used = jnp.arange(listed, dtype=jnp.int32) < negative_pair_count[0]
    offsets = jnp.arange(-RANGE, RANGE + 1, dtype=jnp.int32)
    target = (block + offsets) % blocks
    found = jnp.any((pair_blocks[0][None, :] == target[:, None]) & used[None, :], axis=1)
    return found | (offsets == 0)


def solution(mesh):
    chips = mesh.shape["dp"]
    blocks = chips * mesh.shape["cores"]

    def body(queries, passages, positives, pair_blocks, negative_pair_count):
        rows, width = queries.shape
        block = lax.axis_index(("dp", "cores"))
        present = present_pairs(pair_blocks, negative_pair_count, block, blocks)
        bias = jnp.where(present, 0.0, FAR).astype(jnp.float32)
        bias = jnp.broadcast_to(jnp.pad(bias, (0, 16 - SLOTS))[:, None], (16, rows))
        vmem = pl.BlockSpec(memory_space=pltpu.VMEM)
        anywhere = pl.BlockSpec(memory_space=pl.ANY)
        gq, gp, loss = pl.pallas_call(
            functools.partial(kernel, chips),
            out_shape=(
                jax.ShapeDtypeStruct((rows, width), jnp.float32),
                jax.ShapeDtypeStruct((rows, width), jnp.float32),
                jax.ShapeDtypeStruct((2, 8, rows), jnp.float32),
            ),
            in_specs=[anywhere, anywhere, vmem, vmem, vmem],
            out_specs=(vmem, vmem, vmem),
            scratch_shapes=[
                pltpu.VMEM((SLOTS + 1, 2, 2, rows // 2, width), jnp.bfloat16),
                pltpu.VMEM((SLOTS, 2, 2, rows, rows // 2), jnp.float32),
                pltpu.VMEM((2, rows, 1), jnp.float32),
                pltpu.VMEM((2, rows, 1), jnp.float32),
                pltpu.VMEM((SLOTS, 16, rows), jnp.float32),
                pltpu.VMEM((SLOTS, 2, 8, rows), jnp.float32),
                pltpu.SemaphoreType.DMA((4,)),
                pltpu.SemaphoreType.DMA((40,)),
                pltpu.SemaphoreType.DMA((SLOTS + 1, 2, 2)),
                pltpu.SemaphoreType.DMA((SLOTS,)),
                pltpu.SemaphoreType.DMA((SLOTS,)),
                pltpu.SemaphoreType.DMA((SLOTS,)),
                pltpu.SemaphoreType.DMA((SLOTS,)),
            ],
            compiler_params=pltpu.CompilerParams(
                collective_id=0, has_side_effects=True, vmem_limit_bytes=58 * 2**20
            ),
            cost_estimate=pl.CostEstimate(
                flops=36 * 2 * rows * rows * width,
                bytes_accessed=12 * rows * width,
                transcendentals=54 * rows * rows,
            ),
        )(queries, passages, bias, positives.reshape(rows, 1), positives)
        return loss[0, 0:1], loss[1, 0:1], gq, gp

    split = P(("dp", "cores"), None)
    return jax.shard_map(
        body,
        mesh=mesh,
        in_specs=(split, split, split, split, P(("dp", "cores"))),
        out_specs=(split, split, split, split),
        check_vma=False,
    )
```

```python
import functools

import jax
import jax.numpy as jnp
from jax import lax
from jax.experimental import pallas as pl
from jax.experimental.pallas import tpu as pltpu
from jax.sharding import PartitionSpec as P

RANGE = 4
OWN = RANGE
SLOTS = 2 * RANGE + 1
PASSING = SLOTS
MESH = pl.DeviceIdType.MESH
SCALE = 20.0
LOG2E = 1.4426950408889634
LOG2_SCALE = 4.321928094887363
FAR = -1.0e30

NT = (((1,), (1,)), ((), ()))


def kernel(chips, q_hbm, p_hbm, bias_ref, pos_row, gq_ref, gp_ref, loss_ref,
           buf, sc, weights, tops, totals, bbuf, lbuf,
           load_sem, send_sem, recv_sem, bsend, brecv, lsend, lrecv):
    chip = lax.axis_index("dp")
    core = lax.axis_index("cores")
    me = 2 * chip + core
    blocks = 2 * chips
    j = chip % 4
    sigma = 1 - 2 * (j // 2)
    corner = ((j + 1) // 2) % 2 == 0
    tau = jnp.where(corner, sigma, -sigma)
    across = j // 2

    def device(block):
        block = (block + blocks) % blocks
        return (block // 2, block % 2)

    sibling = (chip, 1 - core)
    x_dev = ((chip + tau + chips) % chips, core)
    y_dev = ((chip + 2 * sigma + chips) % chips, core)
    z_dev = ((chip + 4 * sigma + chips) % chips, core)

    def at(k):
        return OWN + 2 * k

    xs, ys, zs, fs = at(tau), at(2 * sigma), at(-2 * sigma), at(-tau)
    turn = 1 - 2 * core
    half = buf.shape[3]
    rows = 2 * half

    loads = []
    for m, ref in enumerate((q_hbm, p_hbm)):
        for h in range(2):
            loads.append(pltpu.make_async_copy(
                ref.at[pl.ds(h * half, half)], buf.at[m, OWN, h], load_sem.at[2 * m + h]))
    for load in loads:
        load.start()

    barrier = pltpu.get_barrier_semaphore()
    others = [o for o in range(-RANGE, RANGE + 1) if o != 0]
    greeted = others + [-8, 8]
    for o in greeted:
        pl.semaphore_signal(barrier, inc=1, device_id=device(me + o), device_id_type=MESH)
    bbuf[OWN] = bias_ref[...]
    for load in loads:
        load.wait()
    pl.semaphore_wait(barrier, len(greeted))

    def put(src, dst, to, sent, got):
        return pltpu.make_async_remote_copy(
            src_ref=src, dst_ref=dst, send_sem=sent, recv_sem=got, device_id=to, device_id_type=MESH
        )

    def piece(slot, m, h, to, to_slot, n):
        return put(buf.at[m, slot, h], buf.at[m, to_slot, h], to, send_sem.at[n], recv_sem.at[to_slot, m, h])

    def arrival(slot, m, h):
        return piece(slot, m, h, sibling, slot, 0)

    def bias_copy(o):
        slot = OWN - o
        return put(bbuf.at[OWN], bbuf.at[slot], device(me + o), bsend.at[OWN + o], brecv.at[slot])

    def bias_arrival(slot):
        return put(bbuf.at[slot], bbuf.at[slot], sibling, bsend.at[0], brecv.at[slot])

    def lse_copy(o):
        slot = OWN - o
        return put(lbuf.at[OWN], lbuf.at[slot], device(me + o), lsend.at[OWN + o], lrecv.at[slot])

    def choose(a, b):
        return tuple(jnp.where(corner, u, v) for u, v in zip(a, b))

    x_out = [
        choose((OWN, 1, at(-tau)), (OWN, j - 1, at(-tau))),
        choose((OWN, 0, at(-tau)), (OWN, 2 - j, at(-tau))),
        choose((ys, across, at(sigma)), (zs, 0, at(-sigma))),
    ]
    y_out = [
        choose((OWN, 0, at(-2 * sigma)), (OWN, 2 - j, at(-2 * sigma))),
        choose((OWN, 1, at(-2 * sigma)), (xs, 1, PASSING)),
        choose((xs, across, at(-sigma)), (OWN, j - 1, at(-2 * sigma))),
    ]
    x_in = [
        choose((xs, across), (xs, 1)),
        choose((xs, 1 - across), (xs, 0)),
        choose((fs, 0), (fs, j - 1)),
    ]
    y_in = [
        choose((ys, across), (ys, 0)),
        choose((PASSING, 1), (ys, 1)),
        choose((ys, 1 - across), (fs, 2 - j)),
    ]
    z_in = [
        choose((zs, across), (zs, 0)),
        choose((fs, 1), (zs, 1)),
        choose((zs, 1 - across), (zs, 1)),
    ]

    def pick(groups, i):
        g = i // 2
        return tuple(jnp.where(g == 0, a, jnp.where(g == 1, b, c)) for a, b, c in zip(*groups))

    def x_send(i):
        slot, m, there = pick(x_out, i)
        return piece(slot, m, i % 2, x_dev, there, i)

    def y_send(i):
        slot, m, there = pick(y_out, i)
        return piece(slot, m, i % 2, y_dev, there, 6 + i)

    def z_send(i):
        slot, m = pick(y_in, i)
        there = jnp.where(slot == PASSING, at(-sigma), at(-2 * sigma))
        return piece(slot, m, i % 2, z_dev, there, 12 + i)

    def z_count():
        return jnp.where(corner, 6, 4)

    def shared(slot, step):
        there = slot + step
        return jnp.logical_and(jnp.logical_and(there >= 0, there < SLOTS), slot != PASSING)

    def forward(groups, i, n):
        slot, m = pick(groups, i)
        return shared(slot, -turn), piece(slot, m, i % 2, sibling, jnp.where(shared(slot, -turn), slot - turn, 0), n + i)

    for i in range(2):
        x_send(i).start()
        y_send(i).start()
    for o in others:
        bias_copy(o).start()
    own_s = [piece(OWN, m, h, sibling, OWN - turn, 36 + 2 * m + h) for m in range(2) for h in range(2)]
    for copy in own_s:
        copy.start()

    tops[...] = jnp.full(tops.shape, FAR, jnp.float32)
    totals[...] = jnp.zeros(totals.shape, jnp.float32)

    def score(slot, m, h):
        side = 1 - m
        bias = bbuf[jnp.where(side == 0, OWN, slot), pl.ds(jnp.where(side == 0, slot, SLOTS - 1 - slot), 1), :]
        bias = bias[:, :half]
        left = buf[side, OWN].reshape(rows, buf.shape[4])
        s = (SCALE * LOG2E) * lax.dot_general(
            left, buf[m, slot, h], NT, preferred_element_type=jnp.float32
        ) + bias
        sc[slot, side, h] = s
        old = tops[side]
        top = jnp.maximum(old, jnp.max(s, axis=1, keepdims=True))
        totals[side] = totals[side] * jnp.exp2(old - top) + jnp.sum(jnp.exp2(s - top), axis=1, keepdims=True)
        tops[side] = top

    def own(e, carry):
        score(OWN, e // 2, e % 2)
        return carry

    def beside(e, carry):
        arrival(OWN + turn, e // 2, e % 2).wait_recv()
        score(OWN + turn, e // 2, e % 2)
        return carry

    lax.fori_loop(0, 4, own, 0)
    for o in others:
        bias_arrival(OWN - o).wait_recv()
    lax.fori_loop(0, 4, beside, 0)

    def step(t, carry):
        @pl.when(t < 6)
        def _():
            slot, m = pick(x_in, t)
            arrival(slot, m, t % 2).wait_recv()

            @pl.when(t < 4)
            def _():
                x_send(t + 2).start()

            slot, m = pick(y_in, t)
            arrival(slot, m, t % 2).wait_recv()

            @pl.when(t < z_count())
            def _():
                z_send(t).start()

            @pl.when(t < 4)
            def _():
                y_send(t + 2).start()

            for groups, n in ((x_in, 18), (y_in, 24)):
                used, copy = forward(groups, t, n)

                @pl.when(used)
                def _():
                    copy.start()

        @pl.when(jnp.logical_and(t >= 1, t - 1 < z_count()))
        def _():
            slot, m = pick(z_in, t - 1)
            arrival(slot, m, (t - 1) % 2).wait_recv()
            used, copy = forward(z_in, t - 1, 30)

            @pl.when(used)
            def _():
                copy.start()

        def sub(u, carry):
            link = u % 3
            beside = u // 3
            i = t - beside - jnp.where(link == 2, 1, 0)
            near = jnp.logical_and(i >= 0, i < jnp.where(link == 2, z_count(), 6))
            i = jnp.where(near, i, 0)
            slot, m = (
                jnp.where(link == 0, a, jnp.where(link == 1, b, c))
                for a, b, c in zip(pick(x_in, i), pick(y_in, i), pick(z_in, i))
            )
            moved = jnp.where(beside == 1, turn, 0)
            near = jnp.logical_and(near, shared(slot, moved))
            slot = jnp.where(near, slot + moved, 0)

            @pl.when(near)
            def _():
                @pl.when(beside == 1)
                def _():
                    arrival(slot, m, i % 2).wait_recv()

                score(slot, m, i % 2)

            return carry

        lax.fori_loop(0, 6, sub, 0)
        return carry

    lax.fori_loop(0, 8, step, 0)

    for side in range(2):
        lse = tops[side] + jnp.log2(totals[side]) - LOG2_SCALE
        tops[side] = lse
        lbuf[OWN, side] = jnp.transpose(jnp.broadcast_to(lse, (rows, 128)))[0:8]
    for o in others:
        lse_copy(o).start()

    def columns(start, size):
        return pl.ds(start if isinstance(start, int) else pl.multiple_of(start, 128), size)

    def weigh(slot, side):
        for h in range(2):
            s = sc[slot, side, h]
            w = jnp.exp2(s - tops[side]) + jnp.exp2(s - lbuf[slot, 1 - side, 0:1, pl.ds(h * half, half)])
            weights[side, :, columns(slot * rows + h * half, half)] = w.astype(jnp.bfloat16)

    pos_col = jnp.transpose(jnp.broadcast_to(pos_row[...].astype(jnp.float32), (128, rows)))[:, 0:1].astype(jnp.int32)
    for side in range(2):
        paired = jnp.zeros((rows, 1), jnp.float32)
        for h in range(2):
            s = sc[OWN, side, h]
            part = pl.ds(h * half, half)
            if side == 0:
                hit = pos_col == lax.broadcasted_iota(jnp.int32, s.shape, 1) + h * half
            else:
                hit = pos_row[:, part] == lax.broadcasted_iota(jnp.int32, s.shape, 0)
            e = hit.astype(jnp.float32)
            paired = paired + jnp.sum(s * e, axis=1, keepdims=True)
            w = jnp.exp2(s - tops[side]) + jnp.exp2(s - lbuf[OWN, 1 - side, 0:1, part])
            weights[side, :, columns(OWN * rows + h * half, half)] = (w - 2.0 * SCALE * e).astype(jnp.bfloat16)
        loss = (tops[side] + LOG2_SCALE - paired) / LOG2E
        loss_ref[side] = jnp.transpose(jnp.broadcast_to(loss, (rows, 128)))[0:8]

    for o in others:
        put(lbuf.at[OWN - o], lbuf.at[OWN - o], sibling, lsend.at[0], lrecv.at[OWN - o]).wait_recv()

    def product(side, n):
        cols = columns(n * half, half)
        right = buf[1 - side, pl.ds(0, SLOTS), :, :, cols].reshape(SLOTS * rows, half)
        ref = (gq_ref, gp_ref)[side]
        ref[:, cols] = jnp.dot(weights[side], right, preferred_element_type=jnp.float32)

    def first(t, carry):
        weigh(t + t // RANGE, 0)
        return carry

    def both(n, carry):
        product(0, n)
        for t in range(2):
            t = 2 * n + t
            weigh(t + t // RANGE, 1)
        return carry

    def second(n, carry):
        product(1, n)
        return carry

    lax.fori_loop(0, SLOTS - 1, first, 0)
    lax.fori_loop(0, 4, both, 0)
    lax.fori_loop(0, 4, second, 0)

    for copy in own_s:
        copy.wait_send()

    def sent(i, carry):
        x_send(i).wait_send()
        y_send(i).wait_send()
        for groups, n, count in ((x_in, 18, 6), (y_in, 24, 6), (z_in, 30, z_count())):
            used, copy = forward(groups, i, n)

            @pl.when(jnp.logical_and(used, i < count))
            def _():
                copy.wait_send()

        @pl.when(i < z_count())
        def _():
            z_send(i).wait_send()

        return carry

    lax.fori_loop(0, 6, sent, 0)
    for o in others:
        bias_copy(o).wait_send()
        lse_copy(o).wait_send()


def present_pairs(pair_blocks, negative_pair_count, block, blocks):
    listed = pair_blocks.shape[1]
    used = jnp.arange(listed, dtype=jnp.int32) < negative_pair_count[0]
    offsets = jnp.arange(-RANGE, RANGE + 1, dtype=jnp.int32)
    target = (block + offsets) % blocks
    found = jnp.any((pair_blocks[0][None, :] == target[:, None]) & used[None, :], axis=1)
    return found | (offsets == 0)


def solution(mesh):
    chips = mesh.shape["dp"]
    blocks = chips * mesh.shape["cores"]

    def body(queries, passages, positives, pair_blocks, negative_pair_count):
        rows, width = queries.shape
        block = lax.axis_index(("dp", "cores"))
        present = present_pairs(pair_blocks, negative_pair_count, block, blocks)
        bias = jnp.where(present, 0.0, FAR).astype(jnp.float32)
        bias = jnp.broadcast_to(jnp.pad(bias, (0, 16 - SLOTS))[:, None], (16, rows))
        vmem = pl.BlockSpec(memory_space=pltpu.VMEM)
        anywhere = pl.BlockSpec(memory_space=pl.ANY)
        gq, gp, loss = pl.pallas_call(
            functools.partial(kernel, chips),
            out_shape=(
                jax.ShapeDtypeStruct((rows, width), jnp.float32),
                jax.ShapeDtypeStruct((rows, width), jnp.float32),
                jax.ShapeDtypeStruct((2, 8, rows), jnp.float32),
            ),
            in_specs=[anywhere, anywhere, vmem, vmem],
            out_specs=(vmem, vmem, vmem),
            scratch_shapes=[
                pltpu.VMEM((2, SLOTS + 1, 2, rows // 2, width), jnp.bfloat16),
                pltpu.VMEM((SLOTS, 2, 2, rows, rows // 2), jnp.float32),
                pltpu.VMEM((2, rows, SLOTS * rows), jnp.bfloat16),
                pltpu.VMEM((2, rows, 1), jnp.float32),
                pltpu.VMEM((2, rows, 1), jnp.float32),
                pltpu.VMEM((SLOTS, 16, rows), jnp.float32),
                pltpu.VMEM((SLOTS, 2, 8, rows), jnp.float32),
                pltpu.SemaphoreType.DMA((4,)),
                pltpu.SemaphoreType.DMA((40,)),
                pltpu.SemaphoreType.DMA((SLOTS + 1, 2, 2)),
                pltpu.SemaphoreType.DMA((SLOTS,)),
                pltpu.SemaphoreType.DMA((SLOTS,)),
                pltpu.SemaphoreType.DMA((SLOTS,)),
                pltpu.SemaphoreType.DMA((SLOTS,)),
            ],
            compiler_params=pltpu.CompilerParams(
                collective_id=0, has_side_effects=True, vmem_limit_bytes=60 * 2**20
            ),
            cost_estimate=pl.CostEstimate(
                flops=36 * 2 * rows * rows * width,
                bytes_accessed=12 * rows * width,
                transcendentals=54 * rows * rows,
            ),
        )(queries, passages, bias, positives)
        return loss[0, 0:1], loss[1, 0:1], gq, gp

    split = P(("dp", "cores"), None)
    return jax.shard_map(
        body,
        mesh=mesh,
        in_specs=(split, split, split, split, P(("dp", "cores"))),
        out_specs=(split, split, split, split),
        check_vma=False,
    )
```

```python
import functools

import jax
import jax.numpy as jnp
from jax import lax
from jax.experimental import pallas as pl
from jax.experimental.pallas import tpu as pltpu
from jax.sharding import PartitionSpec as P

RANGE = 4
OWN = RANGE
SLOTS = 2 * RANGE + 1
PASSING = SLOTS
MESH = pl.DeviceIdType.MESH
LANES = 128
SCALE = 20.0
LOG2E = 1.4426950408889634
LOG2_SCALE = 4.321928094887363
FAR = -1.0e30

NT = (((1,), (1,)), ((), ()))


def kernel(chips, q_hbm, p_hbm, bias_ref, pos_row, gq_ref, gp_ref, loss_ref,
           buf, sc, tops, totals, bbuf, lbuf,
           load_sem, send_sem, recv_sem, bsend, brecv, lsend, lrecv):
    chip = lax.axis_index("dp")
    core = lax.axis_index("cores")
    me = 2 * chip + core
    blocks = 2 * chips
    j = chip % 4
    sigma = 1 - 2 * (j // 2)
    corner = ((j + 1) // 2) % 2 == 0
    tau = jnp.where(corner, sigma, -sigma)
    across = j // 2

    def device(block):
        block = (block + blocks) % blocks
        return (block // 2, block % 2)

    sibling = (chip, 1 - core)
    x_dev = ((chip + tau + chips) % chips, core)
    y_dev = ((chip + 2 * sigma + chips) % chips, core)
    z_dev = ((chip + 4 * sigma + chips) % chips, core)

    def at(k):
        return OWN + 2 * k

    xs, ys, zs, fs = at(tau), at(2 * sigma), at(-2 * sigma), at(-tau)
    turn = 1 - 2 * core
    half = buf.shape[3]
    rows = 2 * half

    loads = []
    for m, ref in enumerate((q_hbm, p_hbm)):
        for h in range(2):
            loads.append(pltpu.make_async_copy(
                ref.at[pl.ds(h * half, half)], buf.at[m, OWN, h], load_sem.at[2 * m + h]))
    for load in loads:
        load.start()

    barrier = pltpu.get_barrier_semaphore()
    others = [o for o in range(-RANGE, RANGE + 1) if o != 0]
    greeted = others + [-8, 8]
    for o in greeted:
        pl.semaphore_signal(barrier, inc=1, device_id=device(me + o), device_id_type=MESH)
    bbuf[OWN] = bias_ref[...]
    for load in loads:
        load.wait()
    pl.semaphore_wait(barrier, len(greeted))

    def put(src, dst, to, sent, got):
        return pltpu.make_async_remote_copy(
            src_ref=src, dst_ref=dst, send_sem=sent, recv_sem=got, device_id=to, device_id_type=MESH
        )

    def piece(slot, m, h, to, to_slot, n):
        return put(buf.at[m, slot, h], buf.at[m, to_slot, h], to, send_sem.at[n], recv_sem.at[to_slot, m, h])

    def arrival(slot, m, h):
        return piece(slot, m, h, sibling, slot, 0)

    def bias_copy(o):
        slot = OWN - o
        return put(bbuf.at[OWN], bbuf.at[slot], device(me + o), bsend.at[OWN + o], brecv.at[slot])

    def bias_arrival(slot):
        return put(bbuf.at[slot], bbuf.at[slot], sibling, bsend.at[0], brecv.at[slot])

    def lse_copy(o):
        slot = OWN - o
        return put(lbuf.at[OWN], lbuf.at[slot], device(me + o), lsend.at[OWN + o], lrecv.at[slot])

    def choose(a, b):
        return tuple(jnp.where(corner, u, v) for u, v in zip(a, b))

    x_out = [
        choose((OWN, 1, at(-tau)), (OWN, j - 1, at(-tau))),
        choose((OWN, 0, at(-tau)), (OWN, 2 - j, at(-tau))),
        choose((ys, across, at(sigma)), (zs, 0, at(-sigma))),
    ]
    y_out = [
        choose((OWN, 0, at(-2 * sigma)), (OWN, 2 - j, at(-2 * sigma))),
        choose((OWN, 1, at(-2 * sigma)), (xs, 1, PASSING)),
        choose((xs, across, at(-sigma)), (OWN, j - 1, at(-2 * sigma))),
    ]
    x_in = [
        choose((xs, across), (xs, 1)),
        choose((xs, 1 - across), (xs, 0)),
        choose((fs, 0), (fs, j - 1)),
    ]
    y_in = [
        choose((ys, across), (ys, 0)),
        choose((PASSING, 1), (ys, 1)),
        choose((ys, 1 - across), (fs, 2 - j)),
    ]
    z_in = [
        choose((zs, across), (zs, 0)),
        choose((fs, 1), (zs, 1)),
        choose((zs, 1 - across), (zs, 1)),
    ]

    def pick(groups, i):
        g = i // 2
        return tuple(jnp.where(g == 0, a, jnp.where(g == 1, b, c)) for a, b, c in zip(*groups))

    def x_send(i):
        slot, m, there = pick(x_out, i)
        return piece(slot, m, i % 2, x_dev, there, i)

    def y_send(i):
        slot, m, there = pick(y_out, i)
        return piece(slot, m, i % 2, y_dev, there, 6 + i)

    def z_send(i):
        slot, m = pick(y_in, i)
        there = jnp.where(slot == PASSING, at(-sigma), at(-2 * sigma))
        return piece(slot, m, i % 2, z_dev, there, 12 + i)

    def z_count():
        return jnp.where(corner, 6, 4)

    def shared(slot, step):
        there = slot + step
        return jnp.logical_and(jnp.logical_and(there >= 0, there < SLOTS), slot != PASSING)

    def forward(groups, i, n):
        slot, m = pick(groups, i)
        return shared(slot, -turn), piece(slot, m, i % 2, sibling, jnp.where(shared(slot, -turn), slot - turn, 0), n + i)

    for i in range(2):
        x_send(i).start()
        y_send(i).start()
    for o in others:
        bias_copy(o).start()
    own_s = [piece(OWN, m, h, sibling, OWN - turn, 36 + 2 * m + h) for m in range(2) for h in range(2)]
    for copy in own_s:
        copy.start()

    tops[...] = jnp.full(tops.shape, FAR, jnp.float32)
    totals[...] = jnp.zeros(totals.shape, jnp.float32)

    def score(slot, m, h):
        side = 1 - m
        bias = bbuf[jnp.where(side == 0, OWN, slot), pl.ds(jnp.where(side == 0, slot, SLOTS - 1 - slot), 1), :]
        bias = bias[:, :half]
        right = buf[m, slot, h]
        for r in range(2):
            part = pl.ds(r * half, half)
            s = (SCALE * LOG2E) * lax.dot_general(
                buf[side, OWN, r], right, NT, preferred_element_type=jnp.float32
            ) + bias
            sc[slot, side, h, part, :] = s
            groups = [s[:, c:c + LANES] for c in range(0, half, LANES)]
            old = tops[side, part, :]
            top = functools.reduce(jnp.maximum, groups, old)
            total = totals[side, part, :] * jnp.exp2(old - top)
            totals[side, part, :] = sum((jnp.exp2(g - top) for g in groups), total)
            tops[side, part, :] = top

    def own(e, carry):
        score(OWN, e // 2, e % 2)
        return carry

    def beside(e, carry):
        arrival(OWN + turn, e // 2, e % 2).wait_recv()
        score(OWN + turn, e // 2, e % 2)
        return carry

    lax.fori_loop(0, 4, own, 0)
    for o in others:
        bias_arrival(OWN - o).wait_recv()
    lax.fori_loop(0, 4, beside, 0)

    def step(t, carry):
        @pl.when(t < 6)
        def _():
            slot, m = pick(x_in, t)
            arrival(slot, m, t % 2).wait_recv()

            @pl.when(t < 4)
            def _():
                x_send(t + 2).start()

            slot, m = pick(y_in, t)
            arrival(slot, m, t % 2).wait_recv()

            @pl.when(t < z_count())
            def _():
                z_send(t).start()

            @pl.when(t < 4)
            def _():
                y_send(t + 2).start()

            for groups, n in ((x_in, 18), (y_in, 24)):
                used, copy = forward(groups, t, n)

                @pl.when(used)
                def _():
                    copy.start()

        @pl.when(jnp.logical_and(t >= 1, t - 1 < z_count()))
        def _():
            slot, m = pick(z_in, t - 1)
            arrival(slot, m, (t - 1) % 2).wait_recv()
            used, copy = forward(z_in, t - 1, 30)

            @pl.when(used)
            def _():
                copy.start()

        def sub(u, carry):
            link = u % 3
            beside = u // 3
            i = t - beside - jnp.where(link == 2, 1, 0)
            near = jnp.logical_and(i >= 0, i < jnp.where(link == 2, z_count(), 6))
            i = jnp.where(near, i, 0)
            slot, m = (
                jnp.where(link == 0, a, jnp.where(link == 1, b, c))
                for a, b, c in zip(pick(x_in, i), pick(y_in, i), pick(z_in, i))
            )
            moved = jnp.where(beside == 1, turn, 0)
            near = jnp.logical_and(near, shared(slot, moved))
            slot = jnp.where(near, slot + moved, 0)

            @pl.when(near)
            def _():
                @pl.when(beside == 1)
                def _():
                    arrival(slot, m, i % 2).wait_recv()

                score(slot, m, i % 2)

            return carry

        lax.fori_loop(0, 6, sub, 0)
        return carry

    lax.fori_loop(0, 8, step, 0)

    for side in range(2):
        top = jnp.max(tops[side], axis=1, keepdims=True)
        total = jnp.sum(totals[side] * jnp.exp2(tops[side] - top), axis=1, keepdims=True)
        lse = jnp.broadcast_to(top + jnp.log2(total) - LOG2_SCALE, (rows, LANES))
        tops[side] = lse
        lbuf[OWN, side] = jnp.transpose(lse)[0:8]
    for o in others:
        lse_copy(o).start()

    grads = (gq_ref, gp_ref)

    def weight(slot, side, part):
        s = jnp.concatenate([sc[slot, side, h, part, :] for h in range(2)], axis=1)
        lse = jnp.concatenate([tops[side, part, :]] * (rows // LANES), axis=1)
        return s, jnp.exp2(s - lse) + jnp.exp2(s - lbuf[slot, 1 - side, 0:1, :])

    def product(w, slot, side):
        right = buf[1 - side, slot].reshape(rows, buf.shape[4])
        return jnp.dot(w.astype(jnp.bfloat16), right, preferred_element_type=jnp.float32)

    pos_col = jnp.transpose(jnp.broadcast_to(pos_row[...].astype(jnp.float32), (LANES, rows)))[:, 0:1].astype(jnp.int32)
    for side in range(2):
        for r in range(0, rows, half):
            part = pl.ds(r, half)
            s, w = weight(OWN, side, part)
            if side == 0:
                hit = pos_col[r:r + half] == lax.broadcasted_iota(jnp.int32, s.shape, 1)
            else:
                hit = pos_row[...] == lax.broadcasted_iota(jnp.int32, s.shape, 0) + r
            e = hit.astype(jnp.float32)
            paired = jnp.sum(s * e, axis=1, keepdims=True)
            totals[side, part, :] = (tops[side, part, :] + LOG2_SCALE - paired) / LOG2E
            grads[side][part, :] = product(w - 2.0 * SCALE * e, OWN, side)
        loss_ref[side] = jnp.transpose(totals[side])[0:8]

    def later(t, carry):
        pair = (t, SLOTS - 1 - t)
        for slot in pair:
            put(lbuf.at[slot], lbuf.at[slot], sibling, lsend.at[0], lrecv.at[slot]).wait_recv()
        for side in range(2):
            for r in range(0, rows, half):
                part = pl.ds(r, half)
                terms = [product(weight(slot, side, part)[1], slot, side) for slot in pair]
                grads[side][part, :] += terms[0] + terms[1]
        return carry

    lax.fori_loop(0, RANGE, later, 0)

    for copy in own_s:
        copy.wait_send()

    def sent(i, carry):
        x_send(i).wait_send()
        y_send(i).wait_send()
        for groups, n, count in ((x_in, 18, 6), (y_in, 24, 6), (z_in, 30, z_count())):
            used, copy = forward(groups, i, n)

            @pl.when(jnp.logical_and(used, i < count))
            def _():
                copy.wait_send()

        @pl.when(i < z_count())
        def _():
            z_send(i).wait_send()

        return carry

    lax.fori_loop(0, 6, sent, 0)
    for o in others:
        bias_copy(o).wait_send()
        lse_copy(o).wait_send()


def present_pairs(pair_blocks, negative_pair_count, block, blocks):
    listed = pair_blocks.shape[1]
    used = jnp.arange(listed, dtype=jnp.int32) < negative_pair_count[0]
    offsets = jnp.arange(-RANGE, RANGE + 1, dtype=jnp.int32)
    target = (block + offsets) % blocks
    found = jnp.any((pair_blocks[0][None, :] == target[:, None]) & used[None, :], axis=1)
    return found | (offsets == 0)


def solution(mesh):
    chips = mesh.shape["dp"]
    blocks = chips * mesh.shape["cores"]

    def body(queries, passages, positives, pair_blocks, negative_pair_count):
        rows, width = queries.shape
        block = lax.axis_index(("dp", "cores"))
        present = present_pairs(pair_blocks, negative_pair_count, block, blocks)
        bias = jnp.where(present, 0.0, FAR).astype(jnp.float32)
        bias = jnp.broadcast_to(jnp.pad(bias, (0, 16 - SLOTS))[:, None], (16, rows))
        vmem = pl.BlockSpec(memory_space=pltpu.VMEM)
        anywhere = pl.BlockSpec(memory_space=pl.ANY)
        gq, gp, loss = pl.pallas_call(
            functools.partial(kernel, chips),
            out_shape=(
                jax.ShapeDtypeStruct((rows, width), jnp.float32),
                jax.ShapeDtypeStruct((rows, width), jnp.float32),
                jax.ShapeDtypeStruct((2, 8, rows), jnp.float32),
            ),
            in_specs=[anywhere, anywhere, vmem, vmem],
            out_specs=(vmem, vmem, vmem),
            scratch_shapes=[
                pltpu.VMEM((2, SLOTS + 1, 2, rows // 2, width), jnp.bfloat16),
                pltpu.VMEM((SLOTS, 2, 2, rows, rows // 2), jnp.float32),
                pltpu.VMEM((2, rows, LANES), jnp.float32),
                pltpu.VMEM((2, rows, LANES), jnp.float32),
                pltpu.VMEM((SLOTS, 16, rows), jnp.float32),
                pltpu.VMEM((SLOTS, 2, 8, rows), jnp.float32),
                pltpu.SemaphoreType.DMA((4,)),
                pltpu.SemaphoreType.DMA((40,)),
                pltpu.SemaphoreType.DMA((SLOTS + 1, 2, 2)),
                pltpu.SemaphoreType.DMA((SLOTS,)),
                pltpu.SemaphoreType.DMA((SLOTS,)),
                pltpu.SemaphoreType.DMA((SLOTS,)),
                pltpu.SemaphoreType.DMA((SLOTS,)),
            ],
            compiler_params=pltpu.CompilerParams(
                collective_id=0, has_side_effects=True, vmem_limit_bytes=60 * 2**20
            ),
            cost_estimate=pl.CostEstimate(
                flops=36 * 2 * rows * rows * width,
                bytes_accessed=12 * rows * width,
                transcendentals=54 * rows * rows,
            ),
        )(queries, passages, bias, positives)
        return loss[0, 0:1], loss[1, 0:1], gq, gp

    split = P(("dp", "cores"), None)
    return jax.shard_map(
        body,
        mesh=mesh,
        in_specs=(split, split, split, split, P(("dp", "cores"))),
        out_specs=(split, split, split, split),
        check_vma=False,
    )
```

```python
import functools

import jax
import jax.numpy as jnp
from jax import lax
from jax.experimental import pallas as pl
from jax.experimental.pallas import tpu as pltpu
from jax.sharding import PartitionSpec as P

RANGE = 4
OWN = RANGE
SLOTS = 2 * RANGE + 1
PASSING = SLOTS
MESH = pl.DeviceIdType.MESH
LANES = 128
SCALE = 20.0
LOG2E = 1.4426950408889634
LOG2_SCALE = 4.321928094887363
FAR = -1.0e30

NT = (((1,), (1,)), ((), ()))


def kernel(chips, q_hbm, p_hbm, bias_ref, pos_row, gq_ref, gp_ref, loss_ref,
           buf, sc, tops, totals, bbuf, lbuf,
           load_sem, send_sem, recv_sem, bsend, brecv, lsend, lrecv):
    chip = lax.axis_index("dp")
    core = lax.axis_index("cores")
    me = 2 * chip + core
    blocks = 2 * chips
    j = chip % 4
    sigma = 1 - 2 * (j // 2)
    corner = ((j + 1) // 2) % 2 == 0
    tau = jnp.where(corner, sigma, -sigma)
    across = j // 2

    def device(block):
        block = (block + blocks) % blocks
        return (block // 2, block % 2)

    sibling = (chip, 1 - core)
    x_dev = ((chip + tau + chips) % chips, core)
    y_dev = ((chip + 2 * sigma + chips) % chips, core)
    z_dev = ((chip + 4 * sigma + chips) % chips, core)

    def at(k):
        return OWN + 2 * k

    xs, ys, zs, fs = at(tau), at(2 * sigma), at(-2 * sigma), at(-tau)
    turn = 1 - 2 * core
    half = buf.shape[3]
    rows = 2 * half

    loads = []
    for m, ref in enumerate((q_hbm, p_hbm)):
        for h in range(2):
            loads.append(pltpu.make_async_copy(
                ref.at[pl.ds(h * half, half)], buf.at[m, OWN, h], load_sem.at[2 * m + h]))
    for load in loads:
        load.start()

    barrier = pltpu.get_barrier_semaphore()
    others = [o for o in range(-RANGE, RANGE + 1) if o != 0]
    greeted = others + [-8, 8]
    for o in greeted:
        pl.semaphore_signal(barrier, inc=1, device_id=device(me + o), device_id_type=MESH)
    bbuf[OWN] = bias_ref[...]
    for load in loads:
        load.wait()
    pl.semaphore_wait(barrier, len(greeted))

    def put(src, dst, to, sent, got):
        return pltpu.make_async_remote_copy(
            src_ref=src, dst_ref=dst, send_sem=sent, recv_sem=got, device_id=to, device_id_type=MESH
        )

    def piece(slot, m, h, to, to_slot, n):
        return put(buf.at[m, slot, h], buf.at[m, to_slot, h], to, send_sem.at[n], recv_sem.at[to_slot, m, h])

    def arrival(slot, m, h):
        return piece(slot, m, h, sibling, slot, 0)

    def bias_copy(o):
        slot = OWN - o
        return put(bbuf.at[OWN], bbuf.at[slot], device(me + o), bsend.at[OWN + o], brecv.at[slot])

    def bias_arrival(slot):
        return put(bbuf.at[slot], bbuf.at[slot], sibling, bsend.at[0], brecv.at[slot])

    def lse_copy(o):
        slot = OWN - o
        return put(lbuf.at[OWN], lbuf.at[slot], device(me + o), lsend.at[OWN + o], lrecv.at[slot])

    def choose(a, b):
        return tuple(jnp.where(corner, u, v) for u, v in zip(a, b))

    x_out = [
        choose((OWN, 1, at(-tau)), (OWN, j - 1, at(-tau))),
        choose((OWN, 0, at(-tau)), (OWN, 2 - j, at(-tau))),
        choose((ys, across, at(sigma)), (zs, 0, at(-sigma))),
    ]
    y_out = [
        choose((OWN, 0, at(-2 * sigma)), (OWN, 2 - j, at(-2 * sigma))),
        choose((OWN, 1, at(-2 * sigma)), (xs, 1, PASSING)),
        choose((xs, across, at(-sigma)), (OWN, j - 1, at(-2 * sigma))),
    ]
    x_in = [
        choose((xs, across), (xs, 1)),
        choose((xs, 1 - across), (xs, 0)),
        choose((fs, 0), (fs, j - 1)),
    ]
    y_in = [
        choose((ys, across), (ys, 0)),
        choose((PASSING, 1), (ys, 1)),
        choose((ys, 1 - across), (fs, 2 - j)),
    ]
    z_in = [
        choose((zs, across), (zs, 0)),
        choose((fs, 1), (zs, 1)),
        choose((zs, 1 - across), (zs, 1)),
    ]

    def pick(groups, i):
        g = i // 2
        return tuple(jnp.where(g == 0, a, jnp.where(g == 1, b, c)) for a, b, c in zip(*groups))

    def x_send(i):
        slot, m, there = pick(x_out, i)
        return piece(slot, m, i % 2, x_dev, there, i)

    def y_send(i):
        slot, m, there = pick(y_out, i)
        return piece(slot, m, i % 2, y_dev, there, 6 + i)

    def z_send(i):
        slot, m = pick(y_in, i)
        there = jnp.where(slot == PASSING, at(-sigma), at(-2 * sigma))
        return piece(slot, m, i % 2, z_dev, there, 12 + i)

    def z_count():
        return jnp.where(corner, 6, 4)

    def shared(slot, step):
        there = slot + step
        return jnp.logical_and(jnp.logical_and(there >= 0, there < SLOTS), slot != PASSING)

    def forward(groups, i, n):
        slot, m = pick(groups, i)
        return shared(slot, -turn), piece(slot, m, i % 2, sibling, jnp.where(shared(slot, -turn), slot - turn, 0), n + i)

    for i in range(2):
        x_send(i).start()
        y_send(i).start()
    for o in others:
        bias_copy(o).start()
    own_s = [piece(OWN, m, h, sibling, OWN - turn, 36 + 2 * m + h) for m in range(2) for h in range(2)]
    for copy in own_s:
        copy.start()

    tops[...] = jnp.full(tops.shape, FAR, jnp.float32)
    totals[...] = jnp.zeros(totals.shape, jnp.float32)

    def score(slot, m, h):
        side = 1 - m
        bias = bbuf[jnp.where(side == 0, OWN, slot), pl.ds(jnp.where(side == 0, slot, SLOTS - 1 - slot), 1), :]
        bias = bias[:, :half]
        left = buf[side, OWN].reshape(rows, buf.shape[4])
        scores = (SCALE * LOG2E) * lax.dot_general(
            left, buf[m, slot, h], NT, preferred_element_type=jnp.float32
        ) + bias
        sc[slot, side, h] = scores
        for r in range(2):
            part = pl.ds(r * half, half)
            s = scores[r * half:(r + 1) * half]
            groups = [s[:, c:c + LANES] for c in range(0, half, LANES)]
            old = tops[side, part, :]
            top = functools.reduce(jnp.maximum, groups, old)
            total = totals[side, part, :] * jnp.exp2(old - top)
            totals[side, part, :] = sum((jnp.exp2(g - top) for g in groups), total)
            tops[side, part, :] = top

    def own(e, carry):
        score(OWN, e // 2, e % 2)
        return carry

    def beside(e, carry):
        arrival(OWN + turn, e // 2, e % 2).wait_recv()
        score(OWN + turn, e // 2, e % 2)
        return carry

    lax.fori_loop(0, 4, own, 0)
    for o in others:
        bias_arrival(OWN - o).wait_recv()
    lax.fori_loop(0, 4, beside, 0)

    def step(t, carry):
        @pl.when(t < 6)
        def _():
            slot, m = pick(x_in, t)
            arrival(slot, m, t % 2).wait_recv()

            @pl.when(t < 4)
            def _():
                x_send(t + 2).start()

            slot, m = pick(y_in, t)
            arrival(slot, m, t % 2).wait_recv()

            @pl.when(t < z_count())
            def _():
                z_send(t).start()

            @pl.when(t < 4)
            def _():
                y_send(t + 2).start()

            for groups, n in ((x_in, 18), (y_in, 24)):
                used, copy = forward(groups, t, n)

                @pl.when(used)
                def _():
                    copy.start()

        @pl.when(jnp.logical_and(t >= 1, t - 1 < z_count()))
        def _():
            slot, m = pick(z_in, t - 1)
            arrival(slot, m, (t - 1) % 2).wait_recv()
            used, copy = forward(z_in, t - 1, 30)

            @pl.when(used)
            def _():
                copy.start()

        def sub(u, carry):
            link = u % 3
            beside = u // 3
            i = t - beside - jnp.where(link == 2, 1, 0)
            near = jnp.logical_and(i >= 0, i < jnp.where(link == 2, z_count(), 6))
            i = jnp.where(near, i, 0)
            slot, m = (
                jnp.where(link == 0, a, jnp.where(link == 1, b, c))
                for a, b, c in zip(pick(x_in, i), pick(y_in, i), pick(z_in, i))
            )
            moved = jnp.where(beside == 1, turn, 0)
            near = jnp.logical_and(near, shared(slot, moved))
            slot = jnp.where(near, slot + moved, 0)

            @pl.when(near)
            def _():
                @pl.when(beside == 1)
                def _():
                    arrival(slot, m, i % 2).wait_recv()

                score(slot, m, i % 2)

            return carry

        lax.fori_loop(0, 6, sub, 0)
        return carry

    lax.fori_loop(0, 8, step, 0)

    for side in range(2):
        top = jnp.max(tops[side], axis=1, keepdims=True)
        total = jnp.sum(totals[side] * jnp.exp2(tops[side] - top), axis=1, keepdims=True)
        lse = jnp.broadcast_to(top + jnp.log2(total) - LOG2_SCALE, (rows, LANES))
        tops[side] = lse
        lbuf[OWN, side] = jnp.transpose(lse)[0:8]
    for o in others:
        lse_copy(o).start()

    grads = (gq_ref, gp_ref)

    def weight(slot, side, part):
        s = jnp.concatenate([sc[slot, side, h, part, :] for h in range(2)], axis=1)
        lse = jnp.concatenate([tops[side, part, :]] * (rows // LANES), axis=1)
        return s, jnp.exp2(s - lse) + jnp.exp2(s - lbuf[slot, 1 - side, 0:1, :])

    def product(w, slot, side):
        right = buf[1 - side, slot].reshape(rows, buf.shape[4])
        return jnp.dot(w.astype(jnp.bfloat16), right, preferred_element_type=jnp.float32)

    pos_col = jnp.transpose(jnp.broadcast_to(pos_row[...].astype(jnp.float32), (LANES, rows)))[:, 0:1].astype(jnp.int32)
    for side in range(2):
        for r in range(0, rows, half):
            part = pl.ds(r, half)
            s, w = weight(OWN, side, part)
            if side == 0:
                hit = pos_col[r:r + half] == lax.broadcasted_iota(jnp.int32, s.shape, 1)
            else:
                hit = pos_row[...] == lax.broadcasted_iota(jnp.int32, s.shape, 0) + r
            e = hit.astype(jnp.float32)
            paired = jnp.sum(s * e, axis=1, keepdims=True)
            totals[side, part, :] = (tops[side, part, :] + LOG2_SCALE - paired) / LOG2E
            grads[side][part, :] = product(w - 2.0 * SCALE * e, OWN, side)
        loss_ref[side] = jnp.transpose(totals[side])[0:8]

    def later(t, carry):
        pair = (t, SLOTS - 1 - t)
        for slot in pair:
            put(lbuf.at[slot], lbuf.at[slot], sibling, lsend.at[0], lrecv.at[slot]).wait_recv()
        for side in range(2):
            ws = [
                jnp.concatenate(
                    [weight(slot, side, pl.ds(r, half))[1].astype(jnp.bfloat16) for r in range(0, rows, half)], axis=0
                )
                for slot in pair
            ]
            for n in range(0, buf.shape[4], rows):
                cols = pl.ds(n, rows)
                terms = [
                    jnp.dot(w, buf[1 - side, slot, :, :, cols].reshape(rows, rows), preferred_element_type=jnp.float32)
                    for w, slot in zip(ws, pair)
                ]
                grads[side][:, cols] += terms[0] + terms[1]
        return carry

    lax.fori_loop(0, RANGE, later, 0)

    for copy in own_s:
        copy.wait_send()

    def sent(i, carry):
        x_send(i).wait_send()
        y_send(i).wait_send()
        for groups, n, count in ((x_in, 18, 6), (y_in, 24, 6), (z_in, 30, z_count())):
            used, copy = forward(groups, i, n)

            @pl.when(jnp.logical_and(used, i < count))
            def _():
                copy.wait_send()

        @pl.when(i < z_count())
        def _():
            z_send(i).wait_send()

        return carry

    lax.fori_loop(0, 6, sent, 0)
    for o in others:
        bias_copy(o).wait_send()
        lse_copy(o).wait_send()


def present_pairs(pair_blocks, negative_pair_count, block, blocks):
    listed = pair_blocks.shape[1]
    used = jnp.arange(listed, dtype=jnp.int32) < negative_pair_count[0]
    offsets = jnp.arange(-RANGE, RANGE + 1, dtype=jnp.int32)
    target = (block + offsets) % blocks
    found = jnp.any((pair_blocks[0][None, :] == target[:, None]) & used[None, :], axis=1)
    return found | (offsets == 0)


def solution(mesh):
    chips = mesh.shape["dp"]
    blocks = chips * mesh.shape["cores"]

    def body(queries, passages, positives, pair_blocks, negative_pair_count):
        rows, width = queries.shape
        block = lax.axis_index(("dp", "cores"))
        present = present_pairs(pair_blocks, negative_pair_count, block, blocks)
        bias = jnp.where(present, 0.0, FAR).astype(jnp.float32)
        bias = jnp.broadcast_to(jnp.pad(bias, (0, 16 - SLOTS))[:, None], (16, rows))
        vmem = pl.BlockSpec(memory_space=pltpu.VMEM)
        anywhere = pl.BlockSpec(memory_space=pl.ANY)
        gq, gp, loss = pl.pallas_call(
            functools.partial(kernel, chips),
            out_shape=(
                jax.ShapeDtypeStruct((rows, width), jnp.float32),
                jax.ShapeDtypeStruct((rows, width), jnp.float32),
                jax.ShapeDtypeStruct((2, 8, rows), jnp.float32),
            ),
            in_specs=[anywhere, anywhere, vmem, vmem],
            out_specs=(vmem, vmem, vmem),
            scratch_shapes=[
                pltpu.VMEM((2, SLOTS + 1, 2, rows // 2, width), jnp.bfloat16),
                pltpu.VMEM((SLOTS, 2, 2, rows, rows // 2), jnp.float32),
                pltpu.VMEM((2, rows, LANES), jnp.float32),
                pltpu.VMEM((2, rows, LANES), jnp.float32),
                pltpu.VMEM((SLOTS, 16, rows), jnp.float32),
                pltpu.VMEM((SLOTS, 2, 8, rows), jnp.float32),
                pltpu.SemaphoreType.DMA((4,)),
                pltpu.SemaphoreType.DMA((40,)),
                pltpu.SemaphoreType.DMA((SLOTS + 1, 2, 2)),
                pltpu.SemaphoreType.DMA((SLOTS,)),
                pltpu.SemaphoreType.DMA((SLOTS,)),
                pltpu.SemaphoreType.DMA((SLOTS,)),
                pltpu.SemaphoreType.DMA((SLOTS,)),
            ],
            compiler_params=pltpu.CompilerParams(
                collective_id=0, has_side_effects=True, vmem_limit_bytes=60 * 2**20
            ),
            cost_estimate=pl.CostEstimate(
                flops=36 * 2 * rows * rows * width,
                bytes_accessed=12 * rows * width,
                transcendentals=54 * rows * rows,
            ),
        )(queries, passages, bias, positives)
        return loss[0, 0:1], loss[1, 0:1], gq, gp

    split = P(("dp", "cores"), None)
    return jax.shard_map(
        body,
        mesh=mesh,
        in_specs=(split, split, split, split, P(("dp", "cores"))),
        out_specs=(split, split, split, split),
        check_vma=False,
    )
```

```python
import functools

import jax
import jax.numpy as jnp
from jax import lax
from jax.experimental import pallas as pl
from jax.experimental.pallas import tpu as pltpu
from jax.sharding import PartitionSpec as P

RANGE = 4
OWN = RANGE
SLOTS = 2 * RANGE + 1
PASSING = SLOTS
MESH = pl.DeviceIdType.MESH
LANES = 128
SCALE = 20.0
LOG2E = 1.4426950408889634
LOG2_SCALE = 4.321928094887363
FAR = -1.0e30

NT = (((1,), (1,)), ((), ()))


def kernel(chips, q_hbm, p_hbm, bias_ref, pos_row, gq_ref, gp_ref, loss_ref,
           buf, sc, tops, totals, bbuf, lbuf,
           load_sem, send_sem, recv_sem, bsend, brecv, lsend, lrecv):
    chip = lax.axis_index("dp")
    core = lax.axis_index("cores")
    me = 2 * chip + core
    blocks = 2 * chips
    j = chip % 4
    sigma = 1 - 2 * (j // 2)
    corner = ((j + 1) // 2) % 2 == 0
    tau = jnp.where(corner, sigma, -sigma)
    across = j // 2

    def device(block):
        block = (block + blocks) % blocks
        return (block // 2, block % 2)

    sibling = (chip, 1 - core)
    x_dev = ((chip + tau + chips) % chips, core)
    y_dev = ((chip + 2 * sigma + chips) % chips, core)
    z_dev = ((chip + 4 * sigma + chips) % chips, core)

    def at(k):
        return OWN + 2 * k

    xs, ys, zs, fs = at(tau), at(2 * sigma), at(-2 * sigma), at(-tau)
    turn = 1 - 2 * core
    half = buf.shape[3]
    rows = 2 * half

    loads = []
    for m, ref in enumerate((q_hbm, p_hbm)):
        for h in range(2):
            loads.append(pltpu.make_async_copy(
                ref.at[pl.ds(h * half, half)], buf.at[m, OWN, h], load_sem.at[2 * m + h]))
    for load in loads:
        load.start()

    barrier = pltpu.get_barrier_semaphore()
    others = [o for o in range(-RANGE, RANGE + 1) if o != 0]
    greeted = others + [-8, 8]
    for o in greeted:
        pl.semaphore_signal(barrier, inc=1, device_id=device(me + o), device_id_type=MESH)
    bbuf[OWN] = bias_ref[...]
    for load in loads:
        load.wait()
    pl.semaphore_wait(barrier, len(greeted))

    def put(src, dst, to, sent, got):
        return pltpu.make_async_remote_copy(
            src_ref=src, dst_ref=dst, send_sem=sent, recv_sem=got, device_id=to, device_id_type=MESH
        )

    def piece(slot, m, h, to, to_slot, n):
        return put(buf.at[m, slot, h], buf.at[m, to_slot, h], to, send_sem.at[n], recv_sem.at[to_slot, m, h])

    def arrival(slot, m, h):
        return piece(slot, m, h, sibling, slot, 0)

    def bias_copy(o):
        slot = OWN - o
        return put(bbuf.at[OWN], bbuf.at[slot], device(me + o), bsend.at[OWN + o], brecv.at[slot])

    def bias_arrival(slot):
        return put(bbuf.at[slot], bbuf.at[slot], sibling, bsend.at[0], brecv.at[slot])

    def lse_copy(o):
        slot = OWN - o
        return put(lbuf.at[OWN], lbuf.at[slot], device(me + o), lsend.at[OWN + o], lrecv.at[slot])

    def choose(a, b):
        return tuple(jnp.where(corner, u, v) for u, v in zip(a, b))

    x_out = [
        choose((OWN, 1, at(-tau)), (OWN, j - 1, at(-tau))),
        choose((OWN, 0, at(-tau)), (OWN, 2 - j, at(-tau))),
        choose((ys, across, at(sigma)), (zs, 0, at(-sigma))),
    ]
    y_out = [
        choose((OWN, 0, at(-2 * sigma)), (OWN, 2 - j, at(-2 * sigma))),
        choose((OWN, 1, at(-2 * sigma)), (xs, 1, PASSING)),
        choose((xs, across, at(-sigma)), (OWN, j - 1, at(-2 * sigma))),
    ]
    x_in = [
        choose((xs, across), (xs, 1)),
        choose((xs, 1 - across), (xs, 0)),
        choose((fs, 0), (fs, j - 1)),
    ]
    y_in = [
        choose((ys, across), (ys, 0)),
        choose((PASSING, 1), (ys, 1)),
        choose((ys, 1 - across), (fs, 2 - j)),
    ]
    z_in = [
        choose((zs, across), (zs, 0)),
        choose((fs, 1), (zs, 1)),
        choose((zs, 1 - across), (zs, 1)),
    ]

    def pick(groups, i):
        g = i // 2
        return tuple(jnp.where(g == 0, a, jnp.where(g == 1, b, c)) for a, b, c in zip(*groups))

    def x_send(i):
        slot, m, there = pick(x_out, i)
        return piece(slot, m, i % 2, x_dev, there, i)

    def y_send(i):
        slot, m, there = pick(y_out, i)
        return piece(slot, m, i % 2, y_dev, there, 6 + i)

    def z_send(i):
        slot, m = pick(y_in, i)
        there = jnp.where(slot == PASSING, at(-sigma), at(-2 * sigma))
        return piece(slot, m, i % 2, z_dev, there, 12 + i)

    def z_count():
        return jnp.where(corner, 6, 4)

    def shared(slot, step):
        there = slot + step
        return jnp.logical_and(jnp.logical_and(there >= 0, there < SLOTS), slot != PASSING)

    def forward(groups, i, n):
        slot, m = pick(groups, i)
        return shared(slot, -turn), piece(slot, m, i % 2, sibling, jnp.where(shared(slot, -turn), slot - turn, 0), n + i)

    for i in range(2):
        x_send(i).start()
        y_send(i).start()
    for o in others:
        bias_copy(o).start()
    own_s = [piece(OWN, m, h, sibling, OWN - turn, 36 + 2 * m + h) for m in range(2) for h in range(2)]
    for copy in own_s:
        copy.start()

    tops[...] = jnp.full(tops.shape, FAR, jnp.float32)
    totals[...] = jnp.zeros(totals.shape, jnp.float32)

    def score(slot, m, h):
        side = 1 - m
        bias = bbuf[jnp.where(side == 0, OWN, slot), pl.ds(jnp.where(side == 0, slot, SLOTS - 1 - slot), 1), :]
        bias = bias[:, :half]
        left = buf[side, OWN].reshape(rows, buf.shape[4])
        scores = (SCALE * LOG2E) * lax.dot_general(
            left, buf[m, slot, h], NT, preferred_element_type=jnp.float32
        ) + bias
        sc[slot, side, h] = scores
        for r in range(2):
            part = pl.ds(r * half, half)
            s = scores[r * half:(r + 1) * half]
            groups = [s[:, c:c + LANES] for c in range(0, half, LANES)]
            old = tops[side, part, :]
            top = functools.reduce(jnp.maximum, groups, old)
            total = totals[side, part, :] * jnp.exp2(old - top)
            totals[side, part, :] = sum((jnp.exp2(g - top) for g in groups), total)
            tops[side, part, :] = top

    def own(e, carry):
        score(OWN, e // 2, e % 2)
        return carry

    def beside(e, carry):
        arrival(OWN + turn, e // 2, e % 2).wait_recv()
        score(OWN + turn, e // 2, e % 2)
        return carry

    lax.fori_loop(0, 4, own, 0)
    for o in others:
        bias_arrival(OWN - o).wait_recv()

    def step(t, carry):
        @pl.when(t < 6)
        def _():
            slot, m = pick(y_in, t)
            arrival(slot, m, t % 2).wait_recv()

            @pl.when(t < z_count())
            def _():
                z_send(t).start()

            slot, m = pick(x_in, t)
            arrival(slot, m, t % 2).wait_recv()

            @pl.when(t < 4)
            def _():
                x_send(t + 2).start()
                y_send(t + 2).start()

            for groups, n in ((x_in, 18), (y_in, 24)):
                used, copy = forward(groups, t, n)

                @pl.when(used)
                def _():
                    copy.start()

        @pl.when(jnp.logical_and(t >= 1, t - 1 < z_count()))
        def _():
            slot, m = pick(z_in, t - 1)
            arrival(slot, m, (t - 1) % 2).wait_recv()
            used, copy = forward(z_in, t - 1, 30)

            @pl.when(used)
            def _():
                copy.start()

        def sub(u, carry):
            link = u % 3
            beside = u // 3
            i = t - beside - jnp.where(link == 2, 1, 0)
            near = jnp.logical_and(i >= 0, i < jnp.where(link == 2, z_count(), 6))
            i = jnp.where(near, i, 0)
            slot, m = (
                jnp.where(link == 0, a, jnp.where(link == 1, b, c))
                for a, b, c in zip(pick(x_in, i), pick(y_in, i), pick(z_in, i))
            )
            moved = jnp.where(beside == 1, turn, 0)
            near = jnp.logical_and(near, shared(slot, moved))
            slot = jnp.where(near, slot + moved, 0)

            @pl.when(near)
            def _():
                @pl.when(beside == 1)
                def _():
                    arrival(slot, m, i % 2).wait_recv()

                score(slot, m, i % 2)

            return carry

        lax.fori_loop(0, 6, sub, 0)

        @pl.when(t < 4)
        def _():
            beside(t, 0)

        return carry

    lax.fori_loop(0, 8, step, 0)

    for side in range(2):
        top = jnp.max(tops[side], axis=1, keepdims=True)
        total = jnp.sum(totals[side] * jnp.exp2(tops[side] - top), axis=1, keepdims=True)
        lse = jnp.broadcast_to(top + jnp.log2(total) - LOG2_SCALE, (rows, LANES))
        tops[side] = lse
        lbuf[OWN, side] = jnp.transpose(lse)[0:8]
    for o in others:
        lse_copy(o).start()

    grads = (gq_ref, gp_ref)

    def weight(slot, side, part):
        s = jnp.concatenate([sc[slot, side, h, part, :] for h in range(2)], axis=1)
        lse = jnp.concatenate([tops[side, part, :]] * (rows // LANES), axis=1)
        return s, jnp.exp2(s - lse) + jnp.exp2(s - lbuf[slot, 1 - side, 0:1, :])

    def product(w, slot, side):
        right = buf[1 - side, slot].reshape(rows, buf.shape[4])
        return jnp.dot(w.astype(jnp.bfloat16), right, preferred_element_type=jnp.float32)

    pos_col = jnp.transpose(jnp.broadcast_to(pos_row[...].astype(jnp.float32), (LANES, rows)))[:, 0:1].astype(jnp.int32)
    for side in range(2):
        for r in range(0, rows, half):
            part = pl.ds(r, half)
            s, w = weight(OWN, side, part)
            if side == 0:
                hit = pos_col[r:r + half] == lax.broadcasted_iota(jnp.int32, s.shape, 1)
            else:
                hit = pos_row[...] == lax.broadcasted_iota(jnp.int32, s.shape, 0) + r
            e = hit.astype(jnp.float32)
            paired = jnp.sum(s * e, axis=1, keepdims=True)
            totals[side, part, :] = (tops[side, part, :] + LOG2_SCALE - paired) / LOG2E
            grads[side][part, :] = product(w - 2.0 * SCALE * e, OWN, side)
        loss_ref[side] = jnp.transpose(totals[side])[0:8]

    def later(t, carry):
        pair = (t, SLOTS - 1 - t)
        for slot in pair:
            put(lbuf.at[slot], lbuf.at[slot], sibling, lsend.at[0], lrecv.at[slot]).wait_recv()
        for side in range(2):
            ws = [
                jnp.concatenate(
                    [weight(slot, side, pl.ds(r, half))[1].astype(jnp.bfloat16) for r in range(0, rows, half)], axis=0
                )
                for slot in pair
            ]
            for n in range(0, buf.shape[4], rows):
                cols = pl.ds(n, rows)
                terms = [
                    jnp.dot(w, buf[1 - side, slot, :, :, cols].reshape(rows, rows), preferred_element_type=jnp.float32)
                    for w, slot in zip(ws, pair)
                ]
                grads[side][:, cols] += terms[0] + terms[1]
        return carry

    lax.fori_loop(0, RANGE, later, 0)

    for copy in own_s:
        copy.wait_send()

    def sent(i, carry):
        x_send(i).wait_send()
        y_send(i).wait_send()
        for groups, n, count in ((x_in, 18, 6), (y_in, 24, 6), (z_in, 30, z_count())):
            used, copy = forward(groups, i, n)

            @pl.when(jnp.logical_and(used, i < count))
            def _():
                copy.wait_send()

        @pl.when(i < z_count())
        def _():
            z_send(i).wait_send()

        return carry

    lax.fori_loop(0, 6, sent, 0)
    for o in others:
        bias_copy(o).wait_send()
        lse_copy(o).wait_send()


def present_pairs(pair_blocks, negative_pair_count, block, blocks):
    listed = pair_blocks.shape[1]
    used = jnp.arange(listed, dtype=jnp.int32) < negative_pair_count[0]
    offsets = jnp.arange(-RANGE, RANGE + 1, dtype=jnp.int32)
    target = (block + offsets) % blocks
    found = jnp.any((pair_blocks[0][None, :] == target[:, None]) & used[None, :], axis=1)
    return found | (offsets == 0)


def solution(mesh):
    chips = mesh.shape["dp"]
    blocks = chips * mesh.shape["cores"]

    def body(queries, passages, positives, pair_blocks, negative_pair_count):
        rows, width = queries.shape
        block = lax.axis_index(("dp", "cores"))
        present = present_pairs(pair_blocks, negative_pair_count, block, blocks)
        bias = jnp.where(present, 0.0, FAR).astype(jnp.float32)
        bias = jnp.broadcast_to(jnp.pad(bias, (0, 16 - SLOTS))[:, None], (16, rows))
        vmem = pl.BlockSpec(memory_space=pltpu.VMEM)
        anywhere = pl.BlockSpec(memory_space=pl.ANY)
        gq, gp, loss = pl.pallas_call(
            functools.partial(kernel, chips),
            out_shape=(
                jax.ShapeDtypeStruct((rows, width), jnp.float32),
                jax.ShapeDtypeStruct((rows, width), jnp.float32),
                jax.ShapeDtypeStruct((2, 8, rows), jnp.float32),
            ),
            in_specs=[anywhere, anywhere, vmem, vmem],
            out_specs=(vmem, vmem, vmem),
            scratch_shapes=[
                pltpu.VMEM((2, SLOTS + 1, 2, rows // 2, width), jnp.bfloat16),
                pltpu.VMEM((SLOTS, 2, 2, rows, rows // 2), jnp.float32),
                pltpu.VMEM((2, rows, LANES), jnp.float32),
                pltpu.VMEM((2, rows, LANES), jnp.float32),
                pltpu.VMEM((SLOTS, 16, rows), jnp.float32),
                pltpu.VMEM((SLOTS, 2, 8, rows), jnp.float32),
                pltpu.SemaphoreType.DMA((4,)),
                pltpu.SemaphoreType.DMA((40,)),
                pltpu.SemaphoreType.DMA((SLOTS + 1, 2, 2)),
                pltpu.SemaphoreType.DMA((SLOTS,)),
                pltpu.SemaphoreType.DMA((SLOTS,)),
                pltpu.SemaphoreType.DMA((SLOTS,)),
                pltpu.SemaphoreType.DMA((SLOTS,)),
            ],
            compiler_params=pltpu.CompilerParams(
                collective_id=0, has_side_effects=True, vmem_limit_bytes=60 * 2**20
            ),
            cost_estimate=pl.CostEstimate(
                flops=36 * 2 * rows * rows * width,
                bytes_accessed=12 * rows * width,
                transcendentals=54 * rows * rows,
            ),
        )(queries, passages, bias, positives)
        return loss[0, 0:1], loss[1, 0:1], gq, gp

    split = P(("dp", "cores"), None)
    return jax.shard_map(
        body,
        mesh=mesh,
        in_specs=(split, split, split, split, P(("dp", "cores"))),
        out_specs=(split, split, split, split),
        check_vma=False,
    )
```
